32 devices in a mesh: energy: 8 (over y, x, core), slab: 4 (over z).
Axes of the slice: x: 2, y: 2, z: 4, core: 2. Of those that a mesh axis runs over, the one named last changes fastest.
Arguments:
- green_lesser: float32 [16, 4, 2, 128, 128], P('energy', 'slab'), may hold values from -6 to 6
- coupling: float32 [4, 4, 3, 2, 128, 128], P(None, 'slab'), may hold values from -0.375 to 0.375
- occupation: float32 [4], replicated, may hold values from 0.2 to 3
- shifts: int32 [4], replicated, may hold values from 1 to 2, as said below
- neighbours: int32 [4, 3], P('slab'), may hold values from 0 to 3, as said below
Outputs:
- self_energy: float32 [16, 4, 2, 128, 128], P('energy', 'slab')
The draws below stay inside these ranges and needn't reach their ends.
Inputs may be any that keep to these rules, and one draw needn't show every extreme that they name: `shifts`: some mode's shift is 1 and some mode's shift is 2. `neighbours`: entry 0 of row i is max(i - 1, 0), entry 2 is min(i + 1, 3), entry 1 lies within one of i.
All inputs are finite; a program needn't handle non-finite values.
Results may differ from the reference program's by a relative error of at most 0.0001.
Values sent between devices are 32-bit elements; how exact they have to be, the bound alone decides.
No kernel may reach another device: no remote copies, remote signals or barrier semaphores. Data moves between devices by JAX's collectives and lax.ppermute only.
A program may use at most 64 MiB of HBM per device.

```python
import math
import jax
import jax.numpy as jnp
from jax import lax

E_DEV = 2
MODES = 4
K = 3
BLK = 128
NE = 16
NB = 4


def draw_shifts(key, part):
    base = jax.random.randint(key, (MODES,), 1, E_DEV + 1)
    order_modes = jax.random.permutation(jax.random.fold_in(key, 7), MODES)
    modes = jnp.arange(MODES)
    base = jnp.where(modes == order_modes[0], 1, base)
    base = jnp.where(modes == order_modes[1], E_DEV, base)
    return base.astype(jnp.int32)


def draw_neighbours(key, part):
    middle = jax.random.randint(key, (NB,), -1, 2)
    rows = jnp.arange(NB)
    offsets = jnp.stack([-jnp.ones_like(middle), middle, jnp.ones_like(middle)], axis=1)
    return jnp.clip(rows[:, None] + offsets, 0, NB - 1).astype(jnp.int32)


def block_scale(own_key, dims, split, low, top_value):
    def one(position, shards_of):
        steps = jax.random.uniform(jax.random.fold_in(jax.random.fold_in(own_key, 6), position), (shards_of,), jnp.float32, low / len(split), top_value / len(split))
        return jnp.repeat(jnp.exp(steps), dims[position] // shards_of).reshape((-1,) + (1,) * (len(dims) - position - 1))

    level = one(*split[0])
    for cut in split[1:]:
        level = level * one(*cut)
    return level


def bell_draw(key, dims, scale, most, cuts=(), kind=jnp.bfloat16):
    loudness = block_scale(key, dims, cuts, -0.22, 0.18) if cuts else 1.0
    drawn = jax.random.normal(key, dims, jnp.float32) * scale * loudness
    return jnp.minimum(jnp.maximum(drawn, -most), most).astype(kind)


def setup_inputs(seed: int = 0) -> dict:
    key_list = jax.random.split(jax.random.key(seed), 6)
    return {
        "green_lesser": bell_draw(key_list[0], (NE, NB, 2, BLK, BLK), 1.0, 6.0, ((0, 8), (1, 4)), jnp.float32),
        "coupling": bell_draw(key_list[1], (MODES, NB, K, 2, BLK, BLK), (2 * BLK) ** -0.5, 0.375, ((1, 4),), jnp.float32),
        "occupation": jnp.clip(jnp.exp(jax.random.uniform(key_list[2], (MODES,), jnp.float32, math.log(0.2), math.log(3.0))), 0.2, 3.0),
        "shifts": draw_shifts(jax.random.fold_in(key_list[5], 71), 0),
        "neighbours": draw_neighbours(jax.random.fold_in(key_list[5], 71), 0),
    }


def precise_matmul(first, second):
    return jnp.matmul(first, second, precision=lax.Precision.HIGHEST)


def complex_product(leading, trailing):
    lead_real, lead_imag = leading[..., 0, :, :], leading[..., 1, :, :]
    trail_real, trail_imag = trailing[..., 0, :, :], trailing[..., 1, :, :]
    real_part = precise_matmul(lead_real, trail_real) - precise_matmul(lead_imag, trail_imag)
    imag_part = precise_matmul(lead_real, trail_imag) + precise_matmul(lead_imag, trail_real)
    return jnp.stack([real_part, imag_part], axis=-3)


def adjoint_product(leading, trailing):
    lead_real, lead_imag = leading[..., 0, :, :], leading[..., 1, :, :]
    trail_real = jnp.swapaxes(trailing[..., 0, :, :], -1, -2)
    trail_imag = jnp.swapaxes(trailing[..., 1, :, :], -1, -2)
    real_part = precise_matmul(lead_real, trail_real) + precise_matmul(lead_imag, trail_imag)
    imag_part = precise_matmul(lead_imag, trail_real) - precise_matmul(lead_real, trail_imag)
    return jnp.stack([real_part, imag_part], axis=-3)


def sandwich(couple, middle):
    return adjoint_product(complex_product(couple, middle), couple)


def reference(green_lesser, coupling, occupation, shifts, neighbours):
    padded = jnp.pad(green_lesser, ((E_DEV, E_DEV), (0, 0), (0, 0), (0, 0), (0, 0)))

    def one_energy(energy):
        summed = jnp.zeros((NB, 2, BLK, BLK), jnp.float32)
        for mode_index in range(MODES):
            shift_now = shifts[mode_index]
            upper_green = lax.dynamic_index_in_dim(padded, energy + E_DEV + shift_now, 0, keepdims=False)
            lower_green = lax.dynamic_index_in_dim(padded, energy + E_DEV - shift_now, 0, keepdims=False)
            weighted = (occupation[mode_index] + 1.0) * upper_green[neighbours] + occupation[mode_index] * lower_green[neighbours]
            summed = summed + jnp.sum(sandwich(coupling[mode_index], weighted), axis=1)
        return summed

    return lax.map(one_energy, jnp.arange(NE, dtype=jnp.int32))
```

```python
import functools

import jax
import jax.numpy as jnp
from jax import lax
from jax.experimental import pallas as pl
from jax.experimental.pallas import tpu as pltpu
from jax.sharding import PartitionSpec as P


def neighbour_pairs(mesh, axis, other, odd):
    count, count_other = mesh.shape[axis], mesh.shape[other]
    axes = tuple(mesh.axis_names)
    pairs = []
    for here in range(count):
        there = here ^ 1 if not odd else ((here + 1) ^ 1) - 1
        for side in range(count_other):
            inside = 0 <= there < count
            source = {axis: here, other: side}
            target = {axis: there, other: side} if inside else {axis: here, other: side ^ 1}
            if target[other] < count_other:
                flat = [at[axes[0]] * mesh.shape[axes[1]] + at[axes[1]] for at in (source, target)]
                pairs.append((flat[0], flat[1]))
    return axes, pairs


def split(value):
    high = value.astype(jnp.bfloat16)
    return high, (value - high.astype(jnp.float32)).astype(jnp.bfloat16)


def product(lead_high, lead_low, trail_high, trail_low, contract):
    dims = (((1,), (contract,)), ((), ()))
    dot = functools.partial(lax.dot_general, dimension_numbers=dims, preferred_element_type=jnp.float32)
    return dot(lead_high, trail_high) + (dot(lead_low, trail_high) + dot(lead_high, trail_low))


def sandwich_kernel(
    shifts_ref, occupation_ref, neighbours_ref, own_ref, even_ref, odd_ref, couple_ref,
    stay_ref, give_even_ref, give_odd_ref,
    embed_high, embed_low, lead_high, lead_low, back_high, back_low, total,
):
    energies, _, _, size, _ = own_ref.shape
    modes, _, blocks = couple_ref.shape[:3]
    here, place = lax.axis_index("slab"), lax.axis_index("energy")
    for source, ref in enumerate((own_ref, even_ref, odd_ref)):
        for energy in range(energies):
            real_high, real_low = split(ref[energy, 0, 0])
            imag_high, imag_low = split(ref[energy, 0, 1])
            for embed, real, imag in ((embed_high, real_high, imag_high), (embed_low, real_low, imag_low)):
                embed[source, energy, :size, :size] = real
                embed[source, energy, :size, size:] = imag
                embed[source, energy, size:, :size] = -imag
                embed[source, energy, size:, size:] = real
    for block in range(blocks):
        for mode in range(modes):
            real_high, real_low = split(couple_ref[mode, 0, block, 0])
            imag_high, imag_low = split(couple_ref[mode, 0, block, 1])
            rows = slice(mode * size, (mode + 1) * size)
            columns = slice(block * 2 * size, block * 2 * size + size)
            others = slice(block * 2 * size + size, (block + 1) * 2 * size)
            for lead, back, real, imag in (
                (lead_high, back_high, real_high, imag_high),
                (lead_low, back_low, real_low, imag_low),
            ):
                lead[block, rows, :size] = real
                lead[block, rows, size:] = imag
                back[mode, :size, columns] = real
                back[mode, :size, others] = imag
                back[mode, size:, columns] = -imag
                back[mode, size:, others] = real
    total[...] = jnp.zeros_like(total)
    middles = [[] for _ in range(energies)]
    for block in range(blocks):
        offset = neighbours_ref[0, block] - here
        ahead = 1 - 2 * lax.rem(here, 2)
        source = jnp.where(offset == 0, 0, jnp.where(offset == ahead, 1, 2))
        for energy in range(energies):
            middles[energy].append(
                product(
                    lead_high[block], lead_low[block],
                    embed_high[source, energy], embed_low[source, energy], 0,
                )
            )
    for mode in range(modes):
        shift, number = shifts_ref[mode], occupation_ref[mode]
        rows = slice(mode * size, (mode + 1) * size)
        stacked = jnp.concatenate(
            [jnp.concatenate([part[rows] for part in middles[energy]], axis=1) for energy in range(energies)], axis=0
        )
        high, low = split(stacked)
        result = product(high, low, back_high[mode], back_low[mode], 1)
        for energy in range(energies):
            part = result[energy * size : (energy + 1) * size]
            total[energy + energies - shift] += (number + 1.0) * part
            total[energy + energies + shift] += number * part
    left_first = lax.rem(place, 2) == 1
    to_even = jnp.where(left_first, 0, 2 * energies)
    to_odd = jnp.where(left_first, 2 * energies, 0)
    for ref, first in ((stay_ref, energies), (give_even_ref, to_even), (give_odd_ref, to_odd)):
        for energy in range(energies):
            value = total[first + energy]
            ref[energy, 0, 0] = value[:, :size]
            ref[energy, 0, 1] = value[:, size:]


def sum_kernel(ends, stay_ref, got_even_ref, got_odd_ref, out_ref):
    place = lax.axis_index("energy")
    inside = jnp.logical_and(place != 0, place != ends)
    out_ref[...] = stay_ref[...] + got_even_ref[...] + jnp.where(inside, got_odd_ref[...], 0.0)


def shards(mesh, green_lesser, coupling, occupation, shifts, neighbours):
    energies, _, _, size, _ = green_lesser.shape
    modes, _, blocks = coupling.shape[:3]
    swap = lambda value, axis, other, odd: lax.ppermute(value, *neighbour_pairs(mesh, axis, other, odd))
    even = swap(green_lesser, "slab", "energy", False)
    odd = swap(green_lesser, "slab", "energy", True)
    whole = pl.BlockSpec(memory_space=pltpu.VMEM)
    scalar = pl.BlockSpec(memory_space=pltpu.SMEM)
    block = jax.ShapeDtypeStruct(green_lesser.shape, jnp.float32)
    stay, give_even, give_odd = pl.pallas_call(
        sandwich_kernel,
        out_shape=[block] * 3,
        in_specs=[scalar] * 3 + [whole] * 4,
        out_specs=[whole] * 3,
        scratch_shapes=[pltpu.VMEM((3, energies, 2 * size, 2 * size), jnp.bfloat16)] * 2
        + [pltpu.VMEM((blocks, modes * size, 2 * size), jnp.bfloat16)] * 2
        + [pltpu.VMEM((modes, 2 * size, blocks * 2 * size), jnp.bfloat16)] * 2
        + [pltpu.VMEM((3 * energies, size, 2 * size), jnp.float32)],
        compiler_params=pltpu.CompilerParams(vmem_limit_bytes=32 << 20),
    )(shifts, occupation, neighbours, green_lesser, even, odd, coupling)
    got_even = swap(give_even, "energy", "slab", False)
    got_odd = swap(give_odd, "energy", "slab", True)
    return pl.pallas_call(
        functools.partial(sum_kernel, mesh.shape["energy"] - 1),
        out_shape=block,
        in_specs=[whole] * 3,
        out_specs=whole,
    )(stay, got_even, got_odd)


def solution(mesh):
    placed = (
        P("energy", "slab", None, None, None),
        P(None, "slab", None, None, None, None),
        P(),
        P(),
        P("slab", None),
    )
    return jax.shard_map(
        functools.partial(shards, mesh),
        mesh=mesh,
        in_specs=placed,
        out_specs=P("energy", "slab", None, None, None),
        check_vma=False,
    )
```

```python
import functools

import jax
import jax.numpy as jnp
from jax import lax
from jax.experimental import pallas as pl
from jax.experimental.pallas import tpu as pltpu
from jax.sharding import PartitionSpec as P

BYTES = 1 << 20


def neighbour_pairs(mesh, axis, other, odd):
    count, count_other = mesh.shape[axis], mesh.shape[other]
    axes = tuple(mesh.axis_names)
    pairs = []
    for here in range(count):
        there = here ^ 1 if not odd else ((here + 1) ^ 1) - 1
        for side in range(count_other):
            inside = 0 <= there < count
            source = {axis: here, other: side}
            target = {axis: there, other: side} if inside else {axis: here, other: side ^ 1}
            if target[other] < count_other:
                flat = [at[axes[0]] * mesh.shape[axes[1]] + at[axes[1]] for at in (source, target)]
                pairs.append((flat[0], flat[1]))
    return axes, pairs


def split(value):
    high = value.astype(jnp.bfloat16)
    return high, (value - high.astype(jnp.float32)).astype(jnp.bfloat16)


def product(lead_high, lead_low, trail_high, trail_low, contract):
    dims = (((1,), (contract,)), ((), ()))
    dot = functools.partial(lax.dot_general, dimension_numbers=dims, preferred_element_type=jnp.float32)
    return dot(lead_high, trail_high) + (dot(lead_low, trail_high) + dot(lead_high, trail_low))


def embed(target, index, real, imag, size):
    for part, (real_part, imag_part) in enumerate(zip(split(real), split(imag))):
        target[*index, part, :size, :size] = real_part
        target[*index, part, :size, size:] = imag_part
        target[*index, part, size:, :size] = -imag_part
        target[*index, part, size:, size:] = real_part


def prepare_kernel(own_ref, couple_ref, own_embed, lead, back):
    energies, _, _, size, _ = own_ref.shape
    modes, _, blocks = couple_ref.shape[:3]
    for energy in range(energies):
        embed(own_embed, (energy,), own_ref[energy, 0, 0], own_ref[energy, 0, 1], size)
    for block in range(blocks):
        for mode in range(modes):
            real, imag = couple_ref[mode, 0, block, 0], couple_ref[mode, 0, block, 1]
            rows = slice(mode * size, (mode + 1) * size)
            for part, (real_part, imag_part) in enumerate(zip(split(real), split(imag))):
                lead[block, part, rows, :size] = real_part
                lead[block, part, rows, size:] = imag_part
            embed(back, (mode, block), real, imag, size)


def energy_at(step, energies):
    return jnp.where(lax.rem(lax.axis_index("energy"), 2) == 0, step, energies - 1 - step)


def sandwich_kernel(
    step, shifts_hbm, occupation_hbm, neighbours_hbm, own_embed, even_ref, odd_ref, lead, back, *rest,
):
    energies, _, _, size, _ = even_ref.shape
    blocks, _, _, _ = lead.shape
    modes = back.shape[0]
    last = step == energies - 1
    if step:
        before, *rest = rest
    if last:
        stay_ref, give_even_ref, give_odd_ref, *rest = rest
    else:
        after, give_odd_ref, *rest = rest
    got_embed, shifts, occupation, neighbours, sems = rest[:5]
    total = rest[5] if last else after
    scalars = [
        pltpu.make_async_copy(source, target, sems.at[index])
        for index, (source, target) in enumerate(
            ((neighbours_hbm, neighbours), (shifts_hbm, shifts), (occupation_hbm, occupation))
        )
    ]
    for copy in scalars:
        copy.start()
    even_place = lax.rem(lax.axis_index("energy"), 2) == 0
    energy = energy_at(step, energies)
    got_embed[0] = own_embed[energy]
    for source, ref in enumerate((even_ref, odd_ref)):
        embed(got_embed, (source + 1,), ref[energy, 0, 0], ref[energy, 0, 1], size)
    if step:
        total[...] = before[...]
    else:
        total[...] = jnp.zeros_like(total)
    for copy in scalars:
        copy.wait()
    here = lax.axis_index("slab")
    ahead = 1 - 2 * lax.rem(here, 2)
    middles = []
    for block in range(blocks):
        offset = neighbours[0, block] - here
        source = jnp.where(offset == 0, 0, jnp.where(offset == ahead, 1, 2))
        middles.append(product(lead[block, 0], lead[block, 1], got_embed[source, 0], got_embed[source, 1], 0))
    for mode in range(modes):
        shift, number = shifts[mode], occupation[mode]
        rows = slice(mode * size, (mode + 1) * size)
        part = 0.0
        for block in range(blocks):
            high, low = split(middles[block][rows])
            part = part + product(high, low, back[mode, block, 0], back[mode, block, 1], 1)
        total[energy + energies - shift] += (number + 1.0) * part
        total[energy + energies + shift] += number * part

    def put(ref, row, slot):
        value = total[slot]
        ref[row, 0, 0] = value[:, :size]
        ref[row, 0, 1] = value[:, size:]

    put(give_odd_ref, 0, jnp.where(even_place, step, 3 * energies - 1 - step))
    if last:
        for row in range(energies):
            put(stay_ref, row, energies + row)
            put(give_even_ref, row, jnp.where(even_place, 2 * energies, 0) + row)


def sum_kernel(ends, stay_ref, got_even_ref, *rest):
    got_odd_refs, out_ref = rest[:-1], rest[-1]
    energies = stay_ref.shape[0]
    place = lax.axis_index("energy")
    inside = jnp.logical_and(place != 0, place != ends)
    out_ref[...] = stay_ref[...] + got_even_ref[...]
    for step, ref in enumerate(got_odd_refs):
        row = jnp.where(lax.rem(place, 2) == 0, energies - 1 - step, step)
        out_ref[row] += jnp.where(inside, ref[0], 0.0)


def shards(mesh, green_lesser, coupling, occupation, shifts, neighbours):
    energies, _, _, size, _ = green_lesser.shape
    modes, _, blocks = coupling.shape[:3]
    swap = lambda value, axis, other, odd: lax.ppermute(value, *neighbour_pairs(mesh, axis, other, odd))
    vmem = pl.BlockSpec(memory_space=pltpu.VMEM)
    hbm = pl.BlockSpec(memory_space=pl.ANY)
    whole = lambda array: pl.BlockSpec(array.shape, lambda: (0,) * array.ndim)
    params = lambda mib: pltpu.CompilerParams(vmem_limit_bytes=mib * BYTES)
    half = lambda *shape: jax.ShapeDtypeStruct(shape, jnp.bfloat16)
    full = lambda *shape: jax.ShapeDtypeStruct(shape, jnp.float32)

    even = swap(green_lesser, "slab", "energy", False)
    odd = swap(green_lesser, "slab", "energy", True)
    own_embed, lead, back = pl.pallas_call(
        prepare_kernel,
        out_shape=[
            half(energies, 2, 2 * size, 2 * size),
            half(blocks, 2, modes * size, 2 * size),
            half(modes, blocks, 2, 2 * size, 2 * size),
        ],
        in_specs=[whole(green_lesser), whole(coupling)],
        out_specs=[vmem] * 3,
        compiler_params=params(8),
        cost_estimate=pl.CostEstimate(flops=0, bytes_accessed=8 * BYTES, transcendentals=0),
    )(green_lesser, coupling)
    totals = (3 * energies, size, 2 * size)
    got_odds = []
    before = []
    for step in range(energies):
        last = step == energies - 1
        give = full(1, *green_lesser.shape[1:])
        results = pl.pallas_call(
            functools.partial(sandwich_kernel, step),
            out_shape=[full(*green_lesser.shape)] * 2 + [give] if last else [full(*totals), give],
            in_specs=[hbm] * 3 + [vmem] * (5 + len(before)),
            out_specs=[vmem] * (3 if last else 2),
            scratch_shapes=[
                pltpu.VMEM((3, 2, 2 * size, 2 * size), jnp.bfloat16),
                pltpu.SMEM(shifts.shape, jnp.int32),
                pltpu.SMEM(occupation.shape, jnp.float32),
                pltpu.SMEM(neighbours.shape, jnp.int32),
                pltpu.SemaphoreType.DMA((3,)),
            ]
            + ([pltpu.VMEM(totals, jnp.float32)] if last else []),
            compiler_params=params(8),
            cost_estimate=pl.CostEstimate(flops=2 * 10**9, bytes_accessed=8 * BYTES, transcendentals=0),
        )(shifts, occupation, neighbours, own_embed, even, odd, lead, back, *before)
        got_odds.append(swap(results[-1], "energy", "slab", True))
        before = [results[0]]
    stay, give_even, _ = results
    got_even = swap(give_even, "energy", "slab", False)
    return pl.pallas_call(
        functools.partial(sum_kernel, mesh.shape["energy"] - 1),
        out_shape=full(*green_lesser.shape),
        in_specs=[vmem] * (2 + energies),
        out_specs=whole(green_lesser),
        compiler_params=params(4),
    )(stay, got_even, *got_odds)


def solution(mesh):
    placed = (
        P("energy", "slab", None, None, None),
        P(None, "slab", None, None, None, None),
        P(),
        P(),
        P("slab", None),
    )
    return jax.shard_map(
        functools.partial(shards, mesh),
        mesh=mesh,
        in_specs=placed,
        out_specs=P("energy", "slab", None, None, None),
        check_vma=False,
    )
```

```python
import functools

import jax
import jax.numpy as jnp
from jax import lax
from jax.experimental import pallas as pl
from jax.experimental.pallas import tpu as pltpu
from jax.sharding import PartitionSpec as P

BYTES = 1 << 20
ROWS = 8


def neighbour_pairs(mesh, axis, other, odd):
    count, count_other = mesh.shape[axis], mesh.shape[other]
    axes = tuple(mesh.axis_names)
    pairs = []
    for here in range(count):
        there = here ^ 1 if not odd else ((here + 1) ^ 1) - 1
        for side in range(count_other):
            inside = 0 <= there < count
            source = {axis: here, other: side}
            target = {axis: there, other: side} if inside else {axis: here, other: side ^ 1}
            if target[other] < count_other:
                flat = [at[axes[0]] * mesh.shape[axes[1]] + at[axes[1]] for at in (source, target)]
                pairs.append((flat[0], flat[1]))
    return axes, pairs


def even_place():
    return lax.rem(lax.axis_index("energy"), 2) == 0


def row_of(number, energies):
    return jnp.where(even_place(), number, energies - 1 - number)


def split(value):
    high = value.astype(jnp.bfloat16)
    return high, (value - high.astype(jnp.float32)).astype(jnp.bfloat16)


def product(lead_high, lead_low, trail_high, trail_low):
    dot = functools.partial(jnp.dot, preferred_element_type=jnp.float32)
    return dot(lead_high, trail_high) + (dot(lead_low, trail_high) + dot(lead_high, trail_low))


def embed(target, index, real, imag, size):
    for part, (real_part, imag_part) in enumerate(zip(split(real), split(imag))):
        target[*index, part, :size, :size] = real_part
        target[*index, part, :size, size:] = imag_part
        target[*index, part, size:, :size] = -imag_part
        target[*index, part, size:, size:] = real_part


def near_kernel(own_ref, near_ref, sem):
    copy = pltpu.make_async_copy(own_ref.at[pl.ds(row_of(0, own_ref.shape[0]), 1)], near_ref, sem)
    copy.start()
    copy.wait()


def prepare_kernel(
    ends, energies, shifts_hbm, occupation_hbm, neighbours_hbm, couple_ref,
    lead, back, is_own, is_even, down, up, foreign_up, shifts, occupation, neighbours, sems,
):
    modes, _, blocks, _, size, _ = couple_ref.shape
    copies = [
        pltpu.make_async_copy(source, target, sems.at[index])
        for index, (source, target) in enumerate(
            ((shifts_hbm, shifts), (occupation_hbm, occupation), (neighbours_hbm, neighbours))
        )
    ]
    for copy in copies:
        copy.start()
    for mode in range(modes):
        for block in range(blocks):
            real, imag = couple_ref[mode, 0, block, 0], couple_ref[mode, 0, block, 1]
            rows = slice(mode * size, (mode + 1) * size)
            for part, (real_part, imag_part) in enumerate(zip(split(real), split(imag))):
                lead[block, part, rows, :size] = real_part
                lead[block, part, rows, size:] = imag_part
            embed(back, (mode, block), real.T, -imag.T, size)
    for copy in copies:
        copy.wait()
    here, place = lax.axis_index("slab"), lax.axis_index("energy")
    ahead = 1 - 2 * lax.rem(here, 2)
    wide = (ROWS, 2 * size)
    for block in range(blocks):
        offset = neighbours[0, block] - here
        is_own[block] = jnp.full(wide, jnp.where(offset == 0, 1.0, 0.0), jnp.float32)
        is_even[block] = jnp.full(wide, jnp.where(offset == ahead, 1.0, 0.0), jnp.float32)
    inside = jnp.logical_and(place != 0, place != ends)
    for mode in range(modes):
        less, more = occupation[mode], occupation[mode] + 1.0
        down_weight = jnp.where(even_place(), more, less)
        up_weight = jnp.where(even_place(), less, more)
        for shift in range(1, energies + 1):
            chosen = shifts[mode] == shift
            for ref, weight in (
                (down, down_weight), (up, up_weight), (foreign_up, jnp.where(inside, up_weight, 0.0)),
            ):
                ref[mode, shift - 1] = jnp.full(wide, jnp.where(chosen, weight, 0.0), jnp.float32)


def scaled(value, weight):
    return (value.reshape(-1, ROWS, value.shape[1]) * weight[None]).reshape(value.shape)


def sandwiches(own, even, odd, is_own, is_even, lead, back, embeds):
    blocks, size = lead.shape[0], lead.shape[3] // 2
    middles = []
    for block in range(blocks):
        take_own = is_own[block][None, :, :size] != 0.0
        take_even = is_even[block][None, :, :size] != 0.0
        tiles = (size // ROWS, ROWS, size)
        parts = [
            jnp.where(
                take_own, own(part).reshape(tiles),
                jnp.where(take_even, even(part).reshape(tiles), odd(part).reshape(tiles)),
            ).reshape(size, size)
            for part in range(2)
        ]
        embed(embeds, (block,), *parts, size)
        middles.append(product(lead[block, 0], lead[block, 1], embeds[block, 0], embeds[block, 1]))
    for mode in range(back.shape[0]):
        rows = slice(mode * size, (mode + 1) * size)
        total = 0.0
        for block in range(blocks):
            high, low = split(middles[block][rows])
            total = total + product(high, low, back[mode, block, 0], back[mode, block, 1])
        yield mode, total


def put(ref, row, value, add=None):
    size = value.shape[0]
    for part in range(2):
        one = value[:, part * size : (part + 1) * size]
        ref[row, 0, part] = one if add is None else add[row, 0, part] + one


def far_kernel(
    own_ref, even_ref, odd_ref, is_own, is_even, down, up, lead, back, give_ref, stay_ref, give_more_ref, embeds
):
    energies, _, _, size, _ = own_ref.shape
    totals = {}
    for number in range(1, energies):
        row = row_of(number, energies)
        reader = lambda ref: lambda part: ref[row, 0, part]
        for mode, value in sandwiches(
            reader(own_ref), reader(even_ref), reader(odd_ref), is_own, is_even, lead, back, embeds
        ):
            for shift in range(1, energies + 1):
                for target, weights in ((number - shift, down), (number + shift, up)):
                    if -energies < target < 2 * energies:
                        totals[target] = totals.get(target, 0.0) + scaled(value, weights[mode, shift - 1])
    zero = jnp.zeros((size, 2 * size), jnp.float32)
    for index in range(energies - 1):
        put(give_ref, index, totals.get(-1 - index, zero))
    for index in range(energies):
        put(stay_ref, index, totals.get(index, zero))
        put(give_more_ref, index, totals.get(energies + index, zero))


def near_far_kernel(
    own_ref, even_ref, odd_ref, is_own, is_even, up, lead, back, stay_before, give_before, stay_ref, give_ref, embeds
):
    energies, _, _, size, _ = own_ref.shape
    row = row_of(0, energies)
    reader = lambda ref: lambda part: ref[row, 0, part]
    totals = {}
    for mode, value in sandwiches(
        reader(own_ref), reader(even_ref), reader(odd_ref), is_own, is_even, lead, back, embeds
    ):
        for shift in range(1, energies + 1):
            totals[shift] = totals.get(shift, 0.0) + scaled(value, up[mode, shift - 1])
    for index in range(energies):
        if index in totals:
            put(stay_ref, index, totals[index], stay_before)
        else:
            stay_ref[index] = stay_before[index]
        if energies + index in totals:
            put(give_ref, index, totals[energies + index], give_before)
        else:
            give_ref[index] = give_before[index]


def foreign_kernel(own_ref, even_ref, odd_ref, is_own, is_even, up, lead, back, before, stay_ref, embeds):
    energies = before.shape[0]
    reader = lambda ref: lambda part: ref[0, 0, part]
    totals = {}
    for mode, value in sandwiches(
        reader(own_ref), reader(even_ref), reader(odd_ref), is_own, is_even, lead, back, embeds
    ):
        for shift in range(1, energies + 1):
            totals[shift] = totals.get(shift, 0.0) + scaled(value, up[mode, shift - 1])
    for index in range(energies):
        put(stay_ref, index, totals[index + 1], before)


def border_kernel(ends, before, got_odd_ref, stay_ref):
    place = lax.axis_index("energy")
    inside = jnp.logical_and(place != 0, place != ends)
    energies = before.shape[0]
    for number in range(energies - 1):
        stay_ref[number] = before[number] + jnp.where(inside, got_odd_ref[number], 0.0)
    stay_ref[energies - 1] = before[energies - 1]


def sum_kernel(stay_ref, got_even_ref, out_ref):
    energies = stay_ref.shape[0]
    for number in range(energies):
        out_ref[row_of(number, energies)] = stay_ref[number] + got_even_ref[energies - 1 - number]


def shards(mesh, green_lesser, coupling, occupation, shifts, neighbours):
    energies, _, _, size, _ = green_lesser.shape
    modes, _, blocks = coupling.shape[:3]
    ends = mesh.shape["energy"] - 1
    swap = lambda value, axis, other, odd: lax.ppermute(value, *neighbour_pairs(mesh, axis, other, odd))
    slabs = lambda value: [swap(value, "slab", "energy", odd) for odd in (False, True)]
    vmem = pl.BlockSpec(memory_space=pltpu.VMEM)
    hbm = pl.BlockSpec(memory_space=pltpu.HBM)
    half = lambda *shape: jax.ShapeDtypeStruct(shape, jnp.bfloat16)
    full = lambda *shape: jax.ShapeDtypeStruct(shape, jnp.float32)
    block = lambda count: full(count, *green_lesser.shape[1:])

    def call(kernel, outs, ins, args, mib, micros, **more):
        return pl.pallas_call(
            kernel,
            out_shape=outs,
            in_specs=ins,
            out_specs=more.pop("out_specs", [vmem] * len(outs)),
            compiler_params=pltpu.CompilerParams(vmem_limit_bytes=mib * BYTES),
            cost_estimate=pl.CostEstimate(flops=micros * 10**9, bytes_accessed=0, transcendentals=0),
            **more,
        )(*args)

    slab_own = slabs(green_lesser)
    (near,) = call(near_kernel, [block(1)], [hbm], [green_lesser], 2, 10, scratch_shapes=[pltpu.SemaphoreType.DMA])
    foreign = swap(near, "energy", "slab", True)
    slab_foreign = slabs(foreign)
    wide = (ROWS, 2 * size)
    lead, back, is_own, is_even, down, up, foreign_up = call(
        functools.partial(prepare_kernel, ends, energies),
        [half(blocks, 2, modes * size, 2 * size), half(modes, blocks, 2, 2 * size, 2 * size)]
        + [full(blocks, *wide)] * 2 + [full(modes, energies, *wide)] * 3,
        [hbm] * 3 + [vmem], [shifts, occupation, neighbours, coupling], 8, 2,
        scratch_shapes=[
            pltpu.SMEM(shifts.shape, jnp.int32),
            pltpu.SMEM(occupation.shape, jnp.float32),
            pltpu.SMEM(neighbours.shape, jnp.int32),
            pltpu.SemaphoreType.DMA((3,)),
        ],
    )
    embeds = [pltpu.VMEM((blocks, 2, 2 * size, 2 * size), jnp.bfloat16)]
    give_odd, stay, give_even = call(
        far_kernel, [block(energies - 1), block(energies), block(energies)], [vmem] * 9,
        [green_lesser, *slab_own, is_own, is_even, down, up, lead, back], 8, 10, scratch_shapes=embeds,
    )
    got_odd = swap(give_odd, "energy", "slab", True)
    stay, give_even = call(
        near_far_kernel, [block(energies)] * 2, [vmem] * 10,
        [green_lesser, *slab_own, is_own, is_even, up, lead, back, stay, give_even], 8, 10, scratch_shapes=embeds,
    )
    got_even = swap(give_even, "energy", "slab", False)
    (stay,) = call(
        foreign_kernel, [block(energies)], [vmem] * 9,
        [foreign, *slab_foreign, is_own, is_even, foreign_up, lead, back, stay], 8, 0, scratch_shapes=embeds,
    )
    (stay,) = call(
        functools.partial(border_kernel, ends), [block(energies)], [vmem] * 2, [stay, got_odd], 2, 10,
    )
    return call(
        sum_kernel, block(energies), [vmem] * 2, [stay, got_even], 4, 1,
        out_specs=pl.BlockSpec(green_lesser.shape, lambda: (0,) * green_lesser.ndim),
    )


def solution(mesh):
    placed = (
        P("energy", "slab", None, None, None),
        P(None, "slab", None, None, None, None),
        P(),
        P(),
        P("slab", None),
    )
    return jax.shard_map(
        functools.partial(shards, mesh),
        mesh=mesh,
        in_specs=placed,
        out_specs=P("energy", "slab", None, None, None),
        check_vma=False,
    )
```

```python
import functools

import jax
import jax.numpy as jnp
import numpy as np
from jax import lax
from jax.experimental import pallas as pl
from jax.experimental.pallas import tpu as pltpu
from jax.sharding import PartitionSpec as P

BYTES = 1 << 20
ROWS = 8


def neighbour_pairs(mesh, axis, odd, other=None):
    count = mesh.shape[axis]
    axes = tuple(mesh.axis_names)
    flat = lambda at: at[axes[0]] * mesh.shape[axes[1]] + at[axes[1]]
    pairs = []
    for place in np.ndindex(*(mesh.shape[name] for name in axes)):
        here = dict(zip(axes, place))
        partner = here[axis] ^ 1 if not odd else ((here[axis] + 1) ^ 1) - 1
        if other is not None and not 0 <= partner < count:
            there = {**here, other: here[other] ^ 1}
        else:
            there = {**here, axis: partner % count}
        pairs.append((flat(here), flat(there)))
    return axes, pairs


def even_place():
    return lax.rem(lax.axis_index("energy"), 2) == 0


def row_of(number, energies):
    return jnp.where(even_place(), number, energies - 1 - number)


def split(value):
    high = value.astype(jnp.bfloat16)
    return high, (value - high.astype(jnp.float32)).astype(jnp.bfloat16)


def product(lead_high, lead_low, trail_high, trail_low):
    dot = functools.partial(jnp.dot, preferred_element_type=jnp.float32)
    return dot(lead_high, trail_high) + (dot(lead_low, trail_high) + dot(lead_high, trail_low))


def embed(target, index, real, imag, size):
    for part, (real_part, imag_part) in enumerate(zip(split(real), split(imag))):
        target[*index, part, :size, :size] = real_part
        target[*index, part, :size, size:] = imag_part
        target[*index, part, size:, :size] = -imag_part
        target[*index, part, size:, size:] = real_part


def near_kernel(own_ref, near_ref, sem):
    copy = pltpu.make_async_copy(own_ref.at[pl.ds(row_of(0, own_ref.shape[0]), 1)], near_ref, sem)
    copy.start()
    copy.wait()


def prepare_kernel(
    ends, energies, shifts_hbm, occupation_hbm, neighbours_hbm, couple_ref,
    lead, back, is_own, is_even, down, up, foreign_up, shifts, occupation, neighbours, sems,
):
    modes, _, blocks, _, size, _ = couple_ref.shape
    copies = [
        pltpu.make_async_copy(source, target, sems.at[index])
        for index, (source, target) in enumerate(
            ((shifts_hbm, shifts), (occupation_hbm, occupation), (neighbours_hbm, neighbours))
        )
    ]
    for copy in copies:
        copy.start()
    for mode in range(modes):
        for block in range(blocks):
            real, imag = couple_ref[mode, 0, block, 0], couple_ref[mode, 0, block, 1]
            rows = slice(mode * size, (mode + 1) * size)
            for part, (real_part, imag_part) in enumerate(zip(split(real), split(imag))):
                lead[block, part, rows, :size] = real_part
                lead[block, part, rows, size:] = imag_part
            embed(back, (mode, block), real.T, -imag.T, size)
    for copy in copies:
        copy.wait()
    here, place = lax.axis_index("slab"), lax.axis_index("energy")
    ahead = 1 - 2 * lax.rem(here, 2)
    wide = (ROWS, 2 * size)
    for block in range(blocks):
        offset = neighbours[0, block] - here
        is_own[block] = jnp.full(wide, jnp.where(offset == 0, 1.0, 0.0), jnp.float32)
        is_even[block] = jnp.full(wide, jnp.where(offset == ahead, 1.0, 0.0), jnp.float32)
    inside = jnp.logical_and(place != 0, place != ends)
    for mode in range(modes):
        less, more = occupation[mode], occupation[mode] + 1.0
        down_weight = jnp.where(even_place(), more, less)
        up_weight = jnp.where(even_place(), less, more)
        for shift in range(1, energies + 1):
            chosen = shifts[mode] == shift
            for ref, weight in (
                (down, down_weight), (up, up_weight), (foreign_up, jnp.where(inside, up_weight, 0.0)),
            ):
                ref[mode, shift - 1] = jnp.full(wide, jnp.where(chosen, weight, 0.0), jnp.float32)


def scaled(value, weight):
    return (value.reshape(-1, ROWS, value.shape[1]) * weight[None]).reshape(value.shape)


def sandwiches(own, even, odd, is_own, is_even, lead, back, embeds):
    blocks, size = lead.shape[0], lead.shape[3] // 2
    middles = []
    for block in range(blocks):
        take_own = is_own[block][None, :, :size] != 0.0
        take_even = is_even[block][None, :, :size] != 0.0
        tiles = (size // ROWS, ROWS, size)
        parts = [
            jnp.where(
                take_own, own(part).reshape(tiles),
                jnp.where(take_even, even(part).reshape(tiles), odd(part).reshape(tiles)),
            ).reshape(size, size)
            for part in range(2)
        ]
        embed(embeds, (block,), *parts, size)
        middles.append(product(lead[block, 0], lead[block, 1], embeds[block, 0], embeds[block, 1]))
    for mode in range(back.shape[0]):
        rows = slice(mode * size, (mode + 1) * size)
        total = 0.0
        for block in range(blocks):
            high, low = split(middles[block][rows])
            total = total + product(high, low, back[mode, block, 0], back[mode, block, 1])
        yield mode, total


def put(ref, row, value, add=None):
    size = value.shape[0]
    for part in range(2):
        one = value[:, part * size : (part + 1) * size]
        ref[row, 0, part] = one if add is None else add[row, 0, part] + one


def far_kernel(
    own_ref, even_ref, odd_ref, is_own, is_even, down, up, lead, back, give_ref, stay_ref, give_more_ref, embeds
):
    energies, _, _, size, _ = own_ref.shape
    totals = {}
    for number in range(1, energies):
        row = row_of(number, energies)
        reader = lambda ref: lambda part: ref[row, 0, part]
        for mode, value in sandwiches(
            reader(own_ref), reader(even_ref), reader(odd_ref), is_own, is_even, lead, back, embeds
        ):
            for shift in range(1, energies + 1):
                for target, weights in ((number - shift, down), (number + shift, up)):
                    if -energies < target < 2 * energies:
                        totals[target] = totals.get(target, 0.0) + scaled(value, weights[mode, shift - 1])
    zero = jnp.zeros((size, 2 * size), jnp.float32)
    for index in range(energies - 1):
        put(give_ref, index, totals.get(-1 - index, zero))
    for index in range(energies):
        put(stay_ref, index, totals.get(index, zero))
        put(give_more_ref, index, totals.get(energies + index, zero))


def pass_kernel(foreign_ref, after_ref, out_ref):
    out_ref[...] = foreign_ref[...]


def near_far_kernel(
    own_ref, even_ref, odd_ref, is_own, is_even, up, lead, back, stay_before, give_before, stay_ref, give_ref, embeds
):
    energies, _, _, size, _ = own_ref.shape
    row = row_of(0, energies)
    reader = lambda ref: lambda part: ref[row, 0, part]
    totals = {}
    for mode, value in sandwiches(
        reader(own_ref), reader(even_ref), reader(odd_ref), is_own, is_even, lead, back, embeds
    ):
        for shift in range(1, energies + 1):
            totals[shift] = totals.get(shift, 0.0) + scaled(value, up[mode, shift - 1])
    for index in range(energies):
        if index in totals:
            put(stay_ref, index, totals[index], stay_before)
        else:
            stay_ref[index] = stay_before[index]
        if energies + index in totals:
            put(give_ref, index, totals[energies + index], give_before)
        else:
            give_ref[index] = give_before[index]


def foreign_kernel(own_ref, even_ref, odd_ref, is_own, is_even, up, lead, back, before, stay_ref, embeds):
    energies = before.shape[0]
    reader = lambda ref: lambda part: ref[0, 0, part]
    totals = {}
    for mode, value in sandwiches(
        reader(own_ref), reader(even_ref), reader(odd_ref), is_own, is_even, lead, back, embeds
    ):
        for shift in range(1, energies + 1):
            totals[shift] = totals.get(shift, 0.0) + scaled(value, up[mode, shift - 1])
    for index in range(energies):
        put(stay_ref, index, totals[index + 1], before)


def border_kernel(ends, before, got_odd_ref, stay_ref):
    place = lax.axis_index("energy")
    inside = jnp.logical_and(place != 0, place != ends)
    energies = before.shape[0]
    for number in range(energies - 1):
        stay_ref[number] = before[number] + jnp.where(inside, got_odd_ref[number], 0.0)
    stay_ref[energies - 1] = before[energies - 1]


def sum_kernel(stay_ref, got_even_ref, out_ref):
    energies = stay_ref.shape[0]
    for number in range(energies):
        out_ref[row_of(number, energies)] = stay_ref[number] + got_even_ref[energies - 1 - number]


def shards(mesh, green_lesser, coupling, occupation, shifts, neighbours):
    energies, _, _, size, _ = green_lesser.shape
    modes, _, blocks = coupling.shape[:3]
    ends = mesh.shape["energy"] - 1
    swap = lambda value, *how: lax.ppermute(value, *neighbour_pairs(mesh, *how))
    slabs = lambda value: [swap(value, "slab", odd, "energy") for odd in (False, True)]
    vmem = pl.BlockSpec(memory_space=pltpu.VMEM)
    hbm = pl.BlockSpec(memory_space=pltpu.HBM)
    half = lambda *shape: jax.ShapeDtypeStruct(shape, jnp.bfloat16)
    full = lambda *shape: jax.ShapeDtypeStruct(shape, jnp.float32)
    block = lambda count: full(count, *green_lesser.shape[1:])

    def call(kernel, outs, ins, args, mib, micros, **more):
        return pl.pallas_call(
            kernel,
            out_shape=outs,
            in_specs=ins,
            out_specs=more.pop("out_specs", [vmem] * len(outs)),
            compiler_params=pltpu.CompilerParams(vmem_limit_bytes=mib * BYTES),
            cost_estimate=pl.CostEstimate(flops=micros * 10**9, bytes_accessed=0, transcendentals=0),
            **more,
        )(*args)

    slab_own = slabs(green_lesser)
    (near,) = call(near_kernel, [block(1)], [hbm], [green_lesser], 2, 10, scratch_shapes=[pltpu.SemaphoreType.DMA])
    foreign = swap(near, "energy", True)
    wide = (ROWS, 2 * size)
    lead, back, is_own, is_even, down, up, foreign_up = call(
        functools.partial(prepare_kernel, ends, energies),
        [half(blocks, 2, modes * size, 2 * size), half(modes, blocks, 2, 2 * size, 2 * size)]
        + [full(blocks, *wide)] * 2 + [full(modes, energies, *wide)] * 3,
        [hbm] * 3 + [vmem], [shifts, occupation, neighbours, coupling], 8, 2,
        scratch_shapes=[
            pltpu.SMEM(shifts.shape, jnp.int32),
            pltpu.SMEM(occupation.shape, jnp.float32),
            pltpu.SMEM(neighbours.shape, jnp.int32),
            pltpu.SemaphoreType.DMA((3,)),
        ],
    )
    embeds = [pltpu.VMEM((blocks, 2, 2 * size, 2 * size), jnp.bfloat16)]
    give_odd, stay, give_even = call(
        far_kernel, [block(energies - 1), block(energies), block(energies)], [vmem] * 9,
        [green_lesser, *slab_own, is_own, is_even, down, up, lead, back], 8, 10, scratch_shapes=embeds,
    )
    (foreign,) = call(pass_kernel, [block(1)], [vmem] * 2, [foreign, stay], 2, 1)
    slab_foreign = slabs(foreign)
    got_odd = swap(give_odd, "energy", True)
    stay, give_even = call(
        near_far_kernel, [block(energies)] * 2, [vmem] * 10,
        [green_lesser, *slab_own, is_own, is_even, up, lead, back, stay, give_even], 8, 10, scratch_shapes=embeds,
    )
    got_even = swap(give_even, "energy", False)
    (stay,) = call(
        foreign_kernel, [block(energies)], [vmem] * 9,
        [foreign, *slab_foreign, is_own, is_even, foreign_up, lead, back, stay], 8, 0, scratch_shapes=embeds,
    )
    (stay,) = call(
        functools.partial(border_kernel, ends), [block(energies)], [vmem] * 2, [stay, got_odd], 2, 10,
    )
    return call(
        sum_kernel, block(energies), [vmem] * 2, [stay, got_even], 4, 1,
        out_specs=pl.BlockSpec(green_lesser.shape, lambda: (0,) * green_lesser.ndim),
    )


def solution(mesh):
    placed = (
        P("energy", "slab", None, None, None),
        P(None, "slab", None, None, None, None),
        P(),
        P(),
        P("slab", None),
    )
    return jax.shard_map(
        functools.partial(shards, mesh),
        mesh=mesh,
        in_specs=placed,
        out_specs=P("energy", "slab", None, None, None),
        check_vma=False,
    )
```

```python
import functools

import jax
import jax.numpy as jnp
import numpy as np
from jax import lax
from jax.experimental import pallas as pl
from jax.experimental.pallas import tpu as pltpu
from jax.sharding import PartitionSpec as P

BYTES = 1 << 20
ROWS = 8


def neighbour_pairs(mesh, axis, odd, other=None):
    count = mesh.shape[axis]
    axes = tuple(mesh.axis_names)
    flat = lambda at: at[axes[0]] * mesh.shape[axes[1]] + at[axes[1]]
    pairs = []
    for place in np.ndindex(*(mesh.shape[name] for name in axes)):
        here = dict(zip(axes, place))
        partner = here[axis] ^ 1 if not odd else ((here[axis] + 1) ^ 1) - 1
        if other is not None and not 0 <= partner < count:
            there = {**here, other: here[other] ^ 1}
        else:
            there = {**here, axis: partner % count}
        pairs.append((flat(here), flat(there)))
    return axes, pairs


def even_place():
    return lax.rem(lax.axis_index("energy"), 2) == 0


def row_of(number, energies):
    return jnp.where(even_place(), number, energies - 1 - number)


def split(value):
    high = value.astype(jnp.bfloat16)
    return high, (value - high.astype(jnp.float32)).astype(jnp.bfloat16)


def product(lead_high, lead_low, trail_high, trail_low):
    dot = functools.partial(jnp.dot, preferred_element_type=jnp.float32)
    return dot(lead_high, trail_high) + (dot(lead_low, trail_high) + dot(lead_high, trail_low))


def embed(target, index, real, imag, size):
    for part, (real_part, imag_part) in enumerate(zip(split(real), split(imag))):
        target[*index, part, :size, :size] = real_part
        target[*index, part, :size, size:] = imag_part
        target[*index, part, size:, :size] = -imag_part
        target[*index, part, size:, size:] = real_part


def pass_kernel(block_ref, out_ref):
    out_ref[...] = block_ref[...]


def prepare_kernel(
    energies, shifts_hbm, occupation_hbm, neighbours_hbm, couple_ref, far_ref,
    lead, back, is_own, is_even, down, up, far_out, shifts, occupation, neighbours, sems,
):
    modes, _, blocks, _, size, _ = couple_ref.shape
    copies = [
        pltpu.make_async_copy(source, target, sems.at[index])
        for index, (source, target) in enumerate(
            ((shifts_hbm, shifts), (occupation_hbm, occupation), (neighbours_hbm, neighbours))
        )
    ]
    for copy in copies:
        copy.start()
    far_out[...] = far_ref[...]
    for mode in range(modes):
        for block in range(blocks):
            real, imag = couple_ref[mode, 0, block, 0], couple_ref[mode, 0, block, 1]
            rows = slice(mode * size, (mode + 1) * size)
            for part, (real_part, imag_part) in enumerate(zip(split(real), split(imag))):
                lead[block, part, rows, :size] = real_part
                lead[block, part, rows, size:] = imag_part
            embed(back, (mode, block), real.T, -imag.T, size)
    for copy in copies:
        copy.wait()
    here = lax.axis_index("slab")
    ahead = 1 - 2 * lax.rem(here, 2)
    wide = (ROWS, 2 * size)
    for block in range(blocks):
        offset = neighbours[0, block] - here
        is_own[block] = jnp.full(wide, jnp.where(offset == 0, 1.0, 0.0), jnp.float32)
        is_even[block] = jnp.full(wide, jnp.where(offset == ahead, 1.0, 0.0), jnp.float32)
    for mode in range(modes):
        less, more = occupation[mode], occupation[mode] + 1.0
        down_weight = jnp.where(even_place(), more, less)
        up_weight = jnp.where(even_place(), less, more)
        for shift in range(1, energies + 1):
            chosen = shifts[mode] == shift
            for ref, weight in ((down, down_weight), (up, up_weight)):
                ref[mode, shift - 1] = jnp.full(wide, jnp.where(chosen, weight, 0.0), jnp.float32)


def scaled(value, weight):
    return (value.reshape(-1, ROWS, value.shape[1]) * weight[None]).reshape(value.shape)


def sandwiches(own, even, odd, is_own, is_even, lead, back, embeds):
    blocks, size = lead.shape[0], lead.shape[3] // 2
    middles = []
    for block in range(blocks):
        take_own = is_own[block][None, :, :size] != 0.0
        take_even = is_even[block][None, :, :size] != 0.0
        tiles = (size // ROWS, ROWS, size)
        parts = [
            jnp.where(
                take_own, own(part).reshape(tiles),
                jnp.where(take_even, even(part).reshape(tiles), odd(part).reshape(tiles)),
            ).reshape(size, size)
            for part in range(2)
        ]
        embed(embeds, (block,), *parts, size)
        middles.append(product(lead[block, 0], lead[block, 1], embeds[block, 0], embeds[block, 1]))
    for mode in range(back.shape[0]):
        rows = slice(mode * size, (mode + 1) * size)
        total = 0.0
        for block in range(blocks):
            high, low = split(middles[block][rows])
            total = total + product(high, low, back[mode, block, 0], back[mode, block, 1])
        yield mode, total


def put(ref, row, value, add=None):
    size = value.shape[0]
    for part in range(2):
        one = value[:, part * size : (part + 1) * size]
        ref[row, 0, part] = one if add is None else add[row, 0, part] + one


def near_kernel(
    own_ref, odd_ref, even_ref, is_own, is_even, down, up, lead, back, give_ref, border_ref, stay_ref, mate_ref, embeds
):
    energies = stay_ref.shape[0]
    reader = lambda ref: lambda part: ref[0, 0, part]
    totals = {}
    for mode, value in sandwiches(
        reader(own_ref), reader(even_ref), reader(odd_ref), is_own, is_even, lead, back, embeds
    ):
        for shift in range(1, energies + 1):
            for target, weights in ((-shift, down), (shift, up)):
                totals[target] = totals.get(target, 0.0) + scaled(value, weights[mode, shift - 1])
    put(give_ref, 0, totals[-energies])
    for index in range(energies - 1):
        put(border_ref, index, totals[-1 - index])
        put(stay_ref, index + 1, totals[index + 1])
    put(mate_ref, 0, totals[energies])


def far_kernel(
    own_ref, odd_ref, even_ref, is_own, is_even, down, up, lead, back, border, stay, mate,
    give_ref, stay_ref, mate_ref, embeds,
):
    energies = stay_ref.shape[0]
    totals = {}
    for number in range(1, energies):
        row = jnp.where(even_place(), number - 1, energies - 1 - number)
        reader = lambda ref: lambda part: ref[row, 0, part]
        for mode, value in sandwiches(
            reader(own_ref), reader(even_ref), reader(odd_ref), is_own, is_even, lead, back, embeds
        ):
            for shift in range(1, energies + 1):
                for target, weights in ((number - shift, down), (number + shift, up)):
                    totals[target] = totals.get(target, 0.0) + scaled(value, weights[mode, shift - 1])
    for index in range(energies - 1):
        put(give_ref, index, totals[-1 - index], border)
    for index in range(energies):
        if index in totals:
            put(stay_ref, index, totals[index], stay if index else None)
        else:
            stay_ref[index] = stay[index]
        put(mate_ref, index, totals[energies + index], None if index else mate)


def first_kernel(ends, stay_ref, got_first_ref, out_ref):
    energies = stay_ref.shape[0]
    place = lax.axis_index("energy")
    inside = jnp.logical_and(place != 0, place != ends)
    for number in range(energies - 1):
        out_ref[number] = stay_ref[number]
    out_ref[energies - 1] = stay_ref[energies - 1] + jnp.where(inside, got_first_ref[0], 0.0)


def sum_kernel(ends, stay_ref, got_rest_ref, got_even_ref, out_ref):
    energies = stay_ref.shape[0]
    place = lax.axis_index("energy")
    inside = jnp.logical_and(place != 0, place != ends)
    for number in range(energies):
        value = stay_ref[number] + got_even_ref[energies - 1 - number]
        if number < energies - 1:
            value += jnp.where(inside, got_rest_ref[number], 0.0)
        out_ref[row_of(number, energies)] = value


def shards(mesh, green_lesser, coupling, occupation, shifts, neighbours):
    energies, _, _, size, _ = green_lesser.shape
    modes, _, blocks = coupling.shape[:3]
    ends = mesh.shape["energy"] - 1
    swap = lambda value, *how: lax.ppermute(value, *neighbour_pairs(mesh, *how))
    slabs = lambda value: [swap(value, "slab", odd, "energy") for odd in (True, False)]
    vmem = pl.BlockSpec(memory_space=pltpu.VMEM)
    hbm = pl.BlockSpec(memory_space=pltpu.HBM)
    half = lambda *shape: jax.ShapeDtypeStruct(shape, jnp.bfloat16)
    full = lambda *shape: jax.ShapeDtypeStruct(shape, jnp.float32)
    block = lambda count: full(count, *green_lesser.shape[1:])

    def call(kernel, outs, ins, args, mib, micros, **more):
        return pl.pallas_call(
            kernel,
            out_shape=outs,
            in_specs=ins,
            out_specs=more.pop("out_specs", [vmem] * len(outs)),
            compiler_params=pltpu.CompilerParams(vmem_limit_bytes=mib * BYTES),
            cost_estimate=pl.CostEstimate(flops=micros * 10**9, bytes_accessed=0, transcendentals=0),
            **more,
        )(*args)

    near = lax.dynamic_slice_in_dim(green_lesser, row_of(0, energies), 1)
    (near,) = call(pass_kernel, [block(1)], [vmem], [near], 2, 10)
    near_slabs = slabs(near)
    near, green_lesser = lax.optimization_barrier((near, green_lesser))
    far = lax.dynamic_slice_in_dim(green_lesser, jnp.where(even_place(), 1, 0), energies - 1)
    wide = (ROWS, 2 * size)
    lead, back, is_own, is_even, down, up, far = call(
        functools.partial(prepare_kernel, energies),
        [half(blocks, 2, modes * size, 2 * size), half(modes, blocks, 2, 2 * size, 2 * size)]
        + [full(blocks, *wide)] * 2 + [full(modes, energies, *wide)] * 2 + [block(energies - 1)],
        [hbm] * 3 + [vmem] * 2, [shifts, occupation, neighbours, coupling, far], 8, 2,
        scratch_shapes=[
            pltpu.SMEM(shifts.shape, jnp.int32),
            pltpu.SMEM(occupation.shape, jnp.float32),
            pltpu.SMEM(neighbours.shape, jnp.int32),
            pltpu.SemaphoreType.DMA((3,)),
        ],
    )
    far_slabs = slabs(far)
    made = [is_own, is_even, down, up, lead, back]
    embeds = [pltpu.VMEM((blocks, 2, 2 * size, 2 * size), jnp.bfloat16)]
    give_first, border, stay, mate = call(
        near_kernel, [block(1), block(energies - 1), block(energies), block(1)], [vmem] * 9,
        [near, *near_slabs, *made], 8, 10, scratch_shapes=embeds,
    )
    got_first = swap(give_first, "energy", True, "slab")
    give_rest, stay, give_even = call(
        far_kernel, [block(energies - 1), block(energies), block(energies)], [vmem] * 12,
        [far, *far_slabs, *made, border, stay, mate], 8, 10, scratch_shapes=embeds,
    )
    got_rest = swap(give_rest, "energy", True, "slab")
    got_even = swap(give_even, "energy", False)
    (stay,) = call(functools.partial(first_kernel, ends), [block(energies)], [vmem] * 2, [stay, got_first], 2, 10)
    return call(
        functools.partial(sum_kernel, ends), block(energies), [vmem] * 3, [stay, got_rest, got_even], 4, 1,
        out_specs=pl.BlockSpec(green_lesser.shape, lambda: (0,) * green_lesser.ndim),
    )


def solution(mesh):
    placed = (
        P("energy", "slab", None, None, None),
        P(None, "slab", None, None, None, None),
        P(),
        P(),
        P("slab", None),
    )
    return jax.shard_map(
        functools.partial(shards, mesh),
        mesh=mesh,
        in_specs=placed,
        out_specs=P("energy", "slab", None, None, None),
        check_vma=False,
    )
```
